128 devices in a mesh: ctx: 16 (over z, x), head: 8 (over y, core).
Axes of the slice: x: 4, y: 4, z: 4, core: 2. Of those that a mesh axis runs over, the one named last changes fastest.
Arguments:
- chosen: bfloat16 [8192, 4096], P('ctx', 'head'), may hold values from -6 to 6
- positions: int32 [8192], P('ctx'), may hold values from -1 to 32767, as said below
- counts: int32 [16], replicated, may hold values from 0 to 512, as said below
- w_router: bfloat16 [4096], replicated, may hold values from -0.09375 to 0.09375
- gain_attn: float32 [4096], replicated, may hold values from 0.5 to 1.5
- query_weight: bfloat16 [4096, 2048], P(None, 'head')
- w_key: bfloat16 [4096, 2048], P(None, 'head')
- w_value: bfloat16 [4096, 2048], P(None, 'head'), may hold values from -0.09375 to 0.09375
- w_out: bfloat16 [2048, 4096], P('head'), may hold values from -1 to 1
- gain_ffn: float32 [4096], replicated, may hold values from 0.5 to 1.5
- w_gate: bfloat16 [4096, 5504], P(None, 'head'), may hold values from -0.09375 to 0.09375
- w_up: bfloat16 [4096, 5504], P(None, 'head'), may hold values from -0.09375 to 0.09375
- w_down: bfloat16 [5504, 4096], P('head'), may hold values from -0.078125 to 0.078125
Outputs:
- updated: bfloat16 [16, 256, 4096], P('ctx', None, 'head')
The draws below stay inside these ranges and needn't reach their ends.
Inputs may be any that keep to these rules, and one draw needn't show every extreme that they name: The counts sum to 4096; some shard has exactly 512. `positions`: for j < counts[c], slot j of shard c holds the global position of that shard's j-th chosen token, strictly increasing in j and within c * 2048 to (c + 1) * 2048 - 1; later slots hold -1.
All inputs are finite; a program needn't handle non-finite values.
Results may differ from the reference program's by a relative error of at most 0.02.
Values may be sent and summed in bfloat16 or wider, within the bound.
A program may use at most 128 MiB of HBM per device.

```python
import math
import jax
import jax.numpy as jnp
from jax import lax

D = 4096
HEADS = 16
HD = 128
FF = 5504
TOK_DEV = 2048
KEEP_DEV = 256
CAP = 512
CHOSEN = 4096
N_CTX = 16


def routing(key):
    base_key = jax.random.fold_in(key, 200)
    order = jax.random.permutation(jax.random.fold_in(base_key, 1), N_CTX).astype(jnp.int32)
    moved = jax.random.randint(jax.random.fold_in(base_key, 2), (N_CTX // 2,), 0, KEEP_DEV + 1).astype(jnp.int32)
    moved = moved.at[0].set(KEEP_DEV)
    change = jnp.zeros((N_CTX,), jnp.int32).at[order[0::2]].add(moved).at[order[1::2]].add(-moved)
    counts = (KEEP_DEV + change).astype(jnp.int32)
    shard_keys = jax.random.split(jax.random.fold_in(base_key, 3), N_CTX)

    def one_shard(shard_key, shard_count, shard_index):
        router_ranking = jax.random.permutation(shard_key, TOK_DEV).astype(jnp.int32)
        picked = (router_ranking < shard_count).astype(jnp.int32)
        ordered = jnp.argsort(1 - picked, stable=True)[:CAP].astype(jnp.int32)
        slot_index = jnp.arange(CAP, dtype=jnp.int32)
        return jnp.where(slot_index < shard_count, shard_index * TOK_DEV + ordered, -1).astype(jnp.int32)
    placed = jax.vmap(one_shard)(shard_keys, counts, jnp.arange(N_CTX, dtype=jnp.int32))
    return (counts, placed.reshape(N_CTX * CAP).astype(jnp.int32))


def draw_counts(key, part):
    drawn = routing(key)
    return drawn[0]


def draw_positions(key, part):
    drawn = routing(key)
    return drawn[1]


def draw_query_weight(key, part):
    key = jax.random.fold_in(key, 1)
    return (jax.random.normal(key, (D, HEADS * HD), jnp.float32) / math.sqrt(D)).astype(jnp.bfloat16)


def draw_w_key(key, part):
    key = jax.random.fold_in(key, 2)
    return (jax.random.normal(key, (D, HEADS * HD), jnp.float32) / math.sqrt(D)).astype(jnp.bfloat16)


def level_of(key, extent, shards, low, top_value):
    def one(axis_at, blocks):
        steps = jax.random.uniform(jax.random.fold_in(jax.random.fold_in(key, 6), axis_at), (blocks,), jnp.float32, low / len(shards), top_value / len(shards))
        return jnp.repeat(jnp.exp(steps), extent[axis_at] // blocks).reshape((-1,) + (1,) * (len(extent) - axis_at - 1))

    loudness = one(*shards[0])
    for cut in shards[1:]:
        loudness = loudness * one(*cut)
    return loudness


def scatter_about(stream_key, extent, deviation, most, pieces=(), held_as=jnp.bfloat16):
    loudness = level_of(stream_key, extent, pieces, -0.22, 0.18) if pieces else 1.0
    array = jax.random.normal(stream_key, extent, jnp.float32) * deviation * loudness
    return jnp.minimum(jnp.maximum(array, -most), most).astype(held_as)


def setup_inputs(seed: int = 0) -> dict:
    keys = jax.random.split(jax.random.key(seed), 14)
    return {
        "chosen": scatter_about(keys[0], (N_CTX * CAP, D), 1.0, 6.0, ((0, 16), (1, 8))),
        "positions": draw_positions(jax.random.fold_in(keys[13], 71), 0),
        "counts": draw_counts(jax.random.fold_in(keys[13], 71), 0),
        "w_router": scatter_about(keys[3], (D,), D ** -0.5, 0.09375),
        "gain_attn": jnp.clip(1.0 + 0.1 * jax.random.normal(keys[4], (D,), jnp.float32), 0.5, 1.5),
        "query_weight": draw_query_weight(jax.random.fold_in(keys[13], 71), 0),
        "w_key": draw_w_key(jax.random.fold_in(keys[13], 71), 0),
        "w_value": scatter_about(keys[7], (D, HEADS * HD), D ** -0.5, 0.09375, ((1, 8),)),
        "w_out": scatter_about(keys[8], (HEADS * HD, D), (HEADS * HD // 64) ** -0.5, 1.0, ((0, 8),)),
        "gain_ffn": jnp.clip(1.0 + 0.1 * jax.random.normal(keys[9], (D,), jnp.float32), 0.5, 1.5),
        "w_gate": scatter_about(keys[10], (D, FF), D ** -0.5, 0.09375, ((1, 8),)),
        "w_up": scatter_about(keys[11], (D, FF), D ** -0.5, 0.09375, ((1, 8),)),
        "w_down": scatter_about(keys[12], (FF, D), FF ** -0.5, 0.078125, ((0, 8),)),
    }


epsilon = 1e-05

def rms_normalize(widened, gain):
    return widened * lax.rsqrt(lax.optimization_barrier(jnp.mean(widened * widened, axis=-1, keepdims=True)) + epsilon) * gain

def reference(chosen, positions, counts, w_router, gain_attn, query_weight, w_key, w_value, w_out, gain_ffn, w_gate, w_up, w_down):
    count_ends = jnp.cumsum(counts).astype(jnp.int32)
    starts = (count_ends - counts).astype(jnp.int32)
    rank_index = jnp.arange(CHOSEN, dtype=jnp.int32)
    owner_shard = lax.optimization_barrier(jnp.sum((rank_index[:, None] >= count_ends[None, :]).astype(jnp.int32), axis=1))
    owner_shard = jnp.minimum(owner_shard, N_CTX - 1).astype(jnp.int32)
    source = (owner_shard * CAP + rank_index - starts[owner_shard]).astype(jnp.int32)
    inputs = chosen[source]
    place = positions[source]
    router = jax.nn.sigmoid(jnp.dot(inputs, w_router, preferred_element_type=jnp.float32))
    widened = inputs.astype(jnp.float32)
    normed = rms_normalize(widened, gain_attn).astype(jnp.bfloat16)
    queries = jnp.dot(normed, query_weight, preferred_element_type=jnp.float32).astype(jnp.bfloat16)
    key_rows = jnp.dot(normed, w_key, preferred_element_type=jnp.float32).astype(jnp.bfloat16)
    value_rows = jnp.dot(normed, w_value, preferred_element_type=jnp.float32).astype(jnp.bfloat16)
    allowed = place[None, :] <= place[:, None]

    def one_head(head_index):
        offset = (head_index * HD).astype(jnp.int32)
        query_head = lax.dynamic_slice_in_dim(queries, offset, HD, 1)
        key_head = lax.dynamic_slice_in_dim(key_rows, offset, HD, 1)
        value_head = lax.dynamic_slice_in_dim(value_rows, offset, HD, 1)
        scores = jnp.dot(query_head, key_head.T, preferred_element_type=jnp.float32) / math.sqrt(HD)
        scores = jnp.where(allowed, scores, -1e+30)
        largest = lax.optimization_barrier(jnp.max(scores, axis=1, keepdims=True))
        exp_terms = jnp.where(allowed, jnp.exp(scores - largest), 0.0)
        denominator = lax.optimization_barrier(jnp.sum(exp_terms, axis=1, keepdims=True))
        mixed = jnp.dot(exp_terms.astype(jnp.bfloat16), value_head, preferred_element_type=jnp.float32) / denominator
        return mixed.astype(jnp.bfloat16)
    heads_out = lax.map(one_head, jnp.arange(HEADS, dtype=jnp.int32))
    attention = jnp.transpose(heads_out, (1, 0, 2)).reshape(CHOSEN, HEADS * HD)
    attn_out = jnp.dot(attention, w_out, preferred_element_type=jnp.float32)
    middle_hidden = widened + attn_out
    normed_ffn = rms_normalize(middle_hidden, gain_ffn).astype(jnp.bfloat16)
    gate_term = jnp.dot(normed_ffn, w_gate, preferred_element_type=jnp.float32)
    up_term = jnp.dot(normed_ffn, w_up, preferred_element_type=jnp.float32)
    hidden = (jax.nn.silu(gate_term) * up_term).astype(jnp.bfloat16)
    ffn_out = jnp.dot(hidden, w_down, preferred_element_type=jnp.float32)
    result = (widened + router[:, None] * (attn_out + ffn_out)).astype(jnp.bfloat16)
    return jnp.transpose(result.reshape(KEEP_DEV, N_CTX, D), (1, 0, 2))
```

```python
import math

import jax
import jax.numpy as jnp
from jax import lax
from jax.experimental import pallas as pl
from jax.experimental.pallas import tpu as pltpu
from jax.sharding import PartitionSpec as P

MESH = pl.DeviceIdType.MESH
F32 = jnp.float32
BF16 = jnp.bfloat16

HD = 128
ROWS = 256
WIDTH = 512
FULL = 4096
HALF = ROWS // 2
EPS = 1e-05
SCORE_SCALE = math.log2(math.e) / math.sqrt(HD)
MASKED = -1e30
FLOOR = -1e29
PACK = 768
PACK_HALF = PACK // 2
OUT_ROWS = HD + 16


def iota(shape, axis):
    return lax.broadcasted_iota(jnp.int32, shape, axis)


def remote(src, dst, send_sem, recv_sem, to):
    return pltpu.make_async_remote_copy(
        src_ref=src,
        dst_ref=dst,
        send_sem=send_sem,
        recv_sem=recv_sem,
        device_id=to,
        device_id_type=MESH,
    )


def rebalance_send(c, h, counts, chosen, send, recv, ssem, rsem):
    begin = jnp.int32(0)
    for i in range(16):
        begin = begin + jnp.where(i < c, counts[i], 0)
    row = iota((512, 1), 0)
    wanted = 16 * (row & 31) + (((row >> 5) - begin) & 15)
    pick = jnp.where(iota((512, 512), 1) == wanted, 1.0, 0.0).astype(BF16)
    send[...] = (
        jnp.dot(pick, chosen[...], preferred_element_type=F32).astype(BF16).reshape(16, 32, WIDTH)
    )


def rebalance_copies(c, h, send, recv, ssem, rsem):
    copies = []
    for d in range(1, 16):
        to = lax.rem(c + d, 16)
        copies.append(remote(send.at[to], recv.at[c], ssem.at[d], rsem.at[d], (to, h)))
    return copies


def rebalance_pick(c, counts, recv, mine):
    col = iota((1, 512), 1)
    source = col >> 5
    turn = col & 31
    target = jnp.full((1, 512), -1, jnp.int32)
    begin = jnp.int32(0)
    for i in range(16):
        slot = ((c - begin) & 15) + 16 * turn
        here = jnp.where(slot < counts[i], (begin + slot) >> 4, -1)
        target = jnp.where(source == i, here, target)
        begin = begin + counts[i]
    pick = jnp.where(iota((ROWS, 512), 0) == target, 1.0, 0.0).astype(BF16)
    mine[...] = jnp.dot(
        pick, recv[...].reshape(512, WIDTH), preferred_element_type=F32
    ).astype(BF16)


class HeadRing:
    def __init__(self, c, h):
        y = lax.div(h, 2)
        k = lax.rem(h, 2)
        right = lax.rem(y + 1, 4)
        left = lax.rem(y + 3, 4)
        far = lax.rem(y + 2, 4)
        self.c = c
        self.own = h
        self.sib = 2 * y + 1 - k
        self.right = 2 * right + k
        self.left = 2 * left + k
        self.far = 2 * far + k
        self.sib_right = 2 * right + 1 - k
        self.sib_left = 2 * left + 1 - k
        self.sib_far = 2 * far + 1 - k


TOP = pl.ds(0, HALF)
BOTTOM = pl.ds(HALF, HALF)
ALL = pl.ds(0, ROWS)


def gather_blocks(ring, buf, ssem, rsem, absorb):
    c = ring.c
    plan = [
        (ring.own, TOP, ring.right, ring.left),
        (ring.own, BOTTOM, ring.left, ring.right),
        (ring.own, BOTTOM, ring.right, ring.left),
        (ring.own, TOP, ring.left, ring.right),
        (ring.own, ALL, ring.sib, ring.sib),
        (ring.left, TOP, ring.right, ring.far),
        (ring.right, BOTTOM, ring.left, ring.far),
        (ring.left, ALL, ring.sib, ring.sib_left),
        (ring.right, ALL, ring.sib, ring.sib_right),
        (ring.far, ALL, ring.sib, ring.sib_far),
    ]

    def message(i):
        block, rows, to, _ = plan[i]
        ref = buf.at[block, rows]
        return remote(ref, ref, ssem.at[i], rsem.at[i], (c, to))

    def arrive(i):
        _, rows, to, block = plan[i]
        ref = buf.at[block, rows]
        remote(ref, ref, ssem.at[i], rsem.at[i], (c, to)).wait_recv()

    for i in range(5):
        message(i).start()

    def step(t, carry):
        @pl.when(t == 1)
        def _():
            arrive(4)

        @pl.when(t == 2)
        def _():
            arrive(0)
            message(5).start()
            arrive(1)
            message(6).start()
            arrive(2)
            message(7).start()

        @pl.when(t == 3)
        def _():
            arrive(3)
            message(8).start()

        @pl.when(t == 4)
        def _():
            arrive(7)

        @pl.when(t == 5)
        def _():
            arrive(8)

        @pl.when(t == 6)
        def _():
            arrive(5)
            arrive(6)
            message(9).start()

        @pl.when(t == 7)
        def _():
            arrive(9)

        order = [
            ring.own,
            ring.sib,
            ring.left,
            ring.right,
            ring.sib_left,
            ring.sib_right,
            ring.far,
            ring.sib_far,
        ]
        block = order[7]
        for at in range(7):
            block = jnp.where(t == at, order[at], block)
        absorb(block)
        return carry

    lax.fori_loop(0, 8, step, 0)
    for i in range(10):
        message(i).wait_send()


def scatter_sums(ring, produce, sib_out, sib_in, far_out, far_in, near_out, near_in, ssem, rsem):
    c = ring.c

    def to_sib(i):
        return remote(sib_out.at[i], sib_in.at[i], ssem.at[i], rsem.at[i], (c, ring.sib))

    def sib_step(i, carry):
        block = jnp.where(
            i == 0,
            ring.sib_far,
            jnp.where(i == 1, ring.sib_right, jnp.where(i == 2, ring.sib_left, ring.sib)),
        )
        sib_out[i] = produce(block).astype(BF16)
        to_sib(i).start()
        return carry

    lax.fori_loop(0, 4, sib_step, 0)

    far_sum = produce(ring.far)
    to_sib(0).wait_recv()
    far_out[...] = (far_sum + sib_in[0].astype(F32)).astype(BF16)
    far_right = remote(far_out.at[TOP], far_in.at[TOP], ssem.at[4], rsem.at[4], (c, ring.right))
    far_left = remote(far_out.at[BOTTOM], far_in.at[BOTTOM], ssem.at[5], rsem.at[5], (c, ring.left))
    far_right.start()
    far_left.start()

    def near(i, side, rows, to):
        return remote(
            near_out.at[side, rows], near_in.at[side, rows], ssem.at[i], rsem.at[i], (c, to)
        )

    right_bottom = near(6, 0, BOTTOM, ring.right)
    left_top = near(7, 1, TOP, ring.left)
    right_top = near(8, 0, TOP, ring.right)
    left_bottom = near(9, 1, BOTTOM, ring.left)

    right_sum = produce(ring.right)
    to_sib(1).wait_recv()
    right_sum = right_sum + sib_in[1].astype(F32)
    near_out[0, BOTTOM] = right_sum[HALF:].astype(BF16)
    right_bottom.start()
    left_sum = produce(ring.left)
    to_sib(2).wait_recv()
    left_sum = left_sum + sib_in[2].astype(F32)
    near_out[1, TOP] = left_sum[:HALF].astype(BF16)
    left_top.start()

    far_right.wait_recv()
    near_out[0, TOP] = (right_sum[:HALF] + far_in[TOP].astype(F32)).astype(BF16)
    right_top.start()
    far_left.wait_recv()
    near_out[1, BOTTOM] = (left_sum[HALF:] + far_in[BOTTOM].astype(F32)).astype(BF16)
    left_bottom.start()

    own_sum = produce(ring.own)
    to_sib(3).wait_recv()
    own_sum = own_sum + sib_in[3].astype(F32)
    right_bottom.wait_recv()
    left_top.wait_recv()
    right_top.wait_recv()
    left_bottom.wait_recv()
    total = own_sum + near_in[0].astype(F32) + near_in[1].astype(F32)
    for i in range(4):
        to_sib(i).wait_send()
    for copy in (far_right, far_left, right_bottom, left_top, right_top, left_bottom):
        copy.wait_send()
    return total


class PackRing:
    def __init__(self, me, device_of, h, buf, ssem, rsem):
        self.me = me
        plus = lax.rem(me + 1, 4)
        minus = lax.rem(me + 3, 4)
        far = lax.rem(me + 2, 4)
        top = pl.ds(0, PACK_HALF)
        bottom = pl.ds(PACK_HALF, PACK_HALF)
        self.plan = [
            (me, top, plus, minus),
            (me, bottom, minus, plus),
            (me, bottom, plus, minus),
            (me, top, minus, plus),
            (minus, top, plus, far),
            (plus, bottom, minus, far),
        ]
        self.device_of, self.h = device_of, h
        self.buf, self.ssem, self.rsem = buf, ssem, rsem

    def message(self, i):
        block, rows, to, _ = self.plan[i]
        ref = self.buf.at[block, rows]
        return remote(ref, ref, self.ssem.at[i], self.rsem.at[i], (self.device_of(to), self.h))

    def arrive(self, i):
        _, rows, to, block = self.plan[i]
        ref = self.buf.at[block, rows]
        remote(ref, ref, self.ssem.at[i], self.rsem.at[i], (self.device_of(to), self.h)).wait_recv()


def split3(value):
    high = value.astype(BF16).astype(F32)
    rest = value - high
    middle = rest.astype(BF16).astype(F32)
    return high, middle, rest - middle


def partial_attention(queries, query_ctx, keys, key_ctx, slot_gap, scores, out):
    largest = jnp.full((1, ROWS), FLOOR, F32)
    for v in range(4):
        tile = dot_rows(keys[v, pl.ds(0, ROWS)], queries)
        tile = jnp.where(slot_gap <= query_ctx - key_ctx(v), tile, MASKED)
        scores[v] = tile
        largest = jnp.maximum(largest, jnp.max(tile, axis=0, keepdims=True))
    total = jnp.zeros((1, ROWS), F32)
    mixed = jnp.zeros((HD, ROWS), F32)
    for v in range(4):
        terms = jnp.exp2(scores[v] - largest)
        total = total + jnp.sum(terms, axis=0, keepdims=True)
        terms = terms.astype(BF16)
        mixed = mixed + jnp.dot(
            keys[v, pl.ds(2 * ROWS, HALF)], terms[:HALF], preferred_element_type=F32
        )
        mixed = mixed + jnp.dot(
            keys[v, pl.ds(2 * ROWS + HALF, HALF)], terms[HALF:], preferred_element_type=F32
        )
    out[pl.ds(0, HD)] = mixed.astype(BF16)
    row = iota((16, ROWS), 0)
    stats = jnp.zeros((16, ROWS), F32)
    for at, piece in enumerate(split3(largest) + split3(total)):
        stats = jnp.where(row == at, piece, stats)
    out[pl.ds(HD, 16)] = stats.astype(BF16)


def merge_attention(parts):
    stats = [parts[i, pl.ds(HD, 16)].astype(F32) for i in range(4)]
    largest = [(s[0:1] + s[1:2]) + s[2:3] for s in stats]
    totals = [(s[3:4] + s[4:5]) + s[5:6] for s in stats]
    top = jnp.maximum(
        jnp.maximum(largest[0], largest[1]), jnp.maximum(largest[2], largest[3])
    )
    denominator = jnp.zeros((1, ROWS), F32)
    mixed = jnp.zeros((HD, ROWS), F32)
    for i in range(4):
        scale = jnp.exp2(largest[i] - top)
        denominator = denominator + scale * totals[i]
        mixed = mixed + scale * parts[i, pl.ds(0, HD)].astype(F32)
    return mixed / denominator


def dot_rows(a, b):
    return lax.dot_general(a, b, (((1,), (1,)), ((), ())), preferred_element_type=F32)


def lane_sum(value):
    return (value[:, 0:128] + value[:, 128:256]) + (value[:, 256:384] + value[:, 384:512])


def block_kernel(
    counts,
    chosen,
    w_router,
    gain_attn,
    wq_hbm,
    wk_hbm,
    wv_hbm,
    wo_hbm,
    gain_ffn,
    wg_hbm,
    wu_hbm,
    wd_hbm,
    out,
    wq,
    wk,
    wv,
    wo,
    wg,
    wu,
    wd,
    swap_out,
    swap_in,
    rows_in,
    rows_mid,
    acc,
    squares,
    logits,
    packs_z,
    packs_x,
    scores,
    parts_out,
    parts_in,
    attention,
    acc_gate,
    acc_up,
    hidden,
    attn_own,
    sib_out,
    sib_in,
    far_out,
    far_in,
    near_out,
    near_in,
    weight_sem,
    swap_ssem,
    swap_rsem,
    gather_ssem,
    gather_rsem,
    pack_ssem,
    pack_rsem,
    part_ssem,
    part_rsem,
    sum_ssem,
    sum_rsem,
):
    c = lax.axis_index("ctx")
    h = lax.axis_index("head")
    z = lax.div(c, 4)
    x = lax.rem(c, 4)
    ring = HeadRing(c, h)

    barrier = pltpu.get_barrier_semaphore()
    for d in range(1, 16):
        pl.semaphore_signal(
            barrier, inc=1, device_id=(lax.rem(c + d, 16), h), device_id_type=MESH
        )
    for to in (ring.right, ring.left, ring.sib):
        pl.semaphore_signal(barrier, inc=1, device_id=(c, to), device_id_type=MESH)

    loads = [
        pltpu.make_async_copy(wq_hbm, wq, weight_sem.at[0]),
        pltpu.make_async_copy(wk_hbm, wk, weight_sem.at[1]),
        pltpu.make_async_copy(wv_hbm, wv, weight_sem.at[2]),
    ]
    for at, (whole, held) in enumerate(((wg_hbm, wg), (wu_hbm, wu))):
        for b in range(8):
            columns = pl.ds(b * WIDTH, WIDTH)
            loads.append(
                pltpu.make_async_copy(whole.at[:, columns], held.at[b], weight_sem.at[3 + 8 * at + b])
            )
    for b in range(8):
        columns = pl.ds(b * WIDTH, WIDTH)
        loads.append(pltpu.make_async_copy(wo_hbm.at[:, columns], wo.at[b], weight_sem.at[19 + b]))
    for b in range(8):
        columns = pl.ds(b * WIDTH, WIDTH)
        loads.append(pltpu.make_async_copy(wd_hbm.at[:, columns], wd.at[b], weight_sem.at[27 + b]))
    for load in loads:
        load.start()

    rebalance_send(c, h, counts, chosen, swap_out, swap_in, swap_ssem, swap_rsem)
    pl.semaphore_wait(barrier, 18)
    swaps = rebalance_copies(c, h, swap_out, swap_in, swap_ssem, swap_rsem)
    for copy in swaps:
        copy.start()
    swap_in[pl.ds(c, 1)] = swap_out[pl.ds(c, 1)]
    for d in range(1, 16):
        landed = swap_in.at[lax.rem(c + 16 - d, 16)]
        remote(landed, landed, swap_ssem.at[d], swap_rsem.at[d], (c, h)).wait_recv()
    rebalance_pick(c, counts, swap_in, rows_in.at[h])
    for copy in swaps:
        copy.wait_send()

    acc[...] = jnp.zeros_like(acc)
    squares[...] = jnp.zeros_like(squares)
    logits[...] = jnp.zeros_like(logits)
    for load in loads[:3]:
        load.wait()

    def absorb_input(block):
        wide = rows_in[block].astype(F32)
        squares[...] += lane_sum(wide * wide)
        logits[...] += lane_sum(wide * w_router[block].astype(F32))
        scaled = (wide * gain_attn[block]).astype(BF16)
        for at, weight in enumerate((wq, wk, wv)):
            columns = pl.ds(at * 2 * HD, 2 * HD)
            acc[:, columns] += jnp.dot(scaled, weight[block], preferred_element_type=F32)

    gather_blocks(ring, rows_in, gather_ssem.at[0], gather_rsem.at[0], absorb_input)

    scale = lax.rsqrt(jnp.sum(squares[...], axis=1, keepdims=True) * (1.0 / FULL) + EPS)
    router = jax.nn.sigmoid(jnp.sum(logits[...], axis=1, keepdims=True))

    for buf, me, mine, other in ((packs_z, z, 0, 1), (packs_x, x, 1, 0)):
        buf[me, pl.ds(0, ROWS)] = (acc[:, pl.ds((2 + mine) * HD, HD)] * scale).astype(BF16)
        buf[me, pl.ds(ROWS, ROWS)] = (
            acc[:, pl.ds(other * HD, HD)] * (scale * SCORE_SCALE)
        ).astype(BF16)
        value = acc[:, pl.ds((4 + mine) * HD, HD)] * scale
        buf[me, pl.ds(2 * ROWS, HALF)] = value[:HALF].T.astype(BF16)
        buf[me, pl.ds(2 * ROWS + HALF, HALF)] = value[HALF:].T.astype(BF16)

    rings = [
        PackRing(z, lambda to: to * 4 + x, h, packs_z, pack_ssem.at[0], pack_rsem.at[0]),
        PackRing(x, lambda to: z * 4 + to, h, packs_x, pack_ssem.at[1], pack_rsem.at[1]),
    ]
    for i in range(4):
        for r in rings:
            r.message(i).start()
    for i in range(2):
        for r in rings:
            r.arrive(i)
            r.message(4 + i).start()
    for i in range(2, 6):
        for r in rings:
            r.arrive(i)

    slot_gap = (iota((ROWS, ROWS), 0) - iota((ROWS, ROWS), 1)) * 16

    def part_copy(head, i, to):
        me = (x, z)[head]
        device = (z * 4 + to, to * 4 + x)[head]
        return remote(
            parts_out.at[head, i],
            parts_in.at[head, me],
            part_ssem.at[head, i],
            part_rsem.at[head, i],
            (device, h),
        )

    def offset_of(i):
        return jnp.where(i == 0, 2, jnp.where(i == 1, 1, jnp.where(i == 2, 3, 0)))

    def attend(i, carry):
        off = offset_of(i)
        to_x = lax.rem(x + off, 4)
        to_z = lax.rem(z + off, 4)
        partial_attention(
            packs_x[to_x, pl.ds(ROWS, ROWS)],
            z * 4 + to_x,
            packs_z,
            lambda v: v * 4 + x,
            slot_gap,
            scores.at[0],
            parts_out.at[0, i],
        )
        partial_attention(
            packs_z[to_z, pl.ds(ROWS, ROWS)],
            to_z * 4 + x,
            packs_x,
            lambda v: z * 4 + v,
            slot_gap,
            scores.at[1],
            parts_out.at[1, i],
        )

        @pl.when(i < 3)
        def _():
            part_copy(0, i, to_x).start()
            part_copy(1, i, to_z).start()

        return carry

    lax.fori_loop(0, 4, attend, 0)
    parts_in[0, pl.ds(x, 1)] = parts_out[0, pl.ds(3, 1)]
    parts_in[1, pl.ds(z, 1)] = parts_out[1, pl.ds(3, 1)]
    for r in rings:
        for i in range(6):
            r.message(i).wait_send()
    for head, me in ((0, x), (1, z)):
        for i, off in enumerate((2, 1, 3)):
            landed = parts_in.at[head, lax.rem(me + 4 - off, 4)]
            remote(
                landed, landed, part_ssem.at[head, i], part_rsem.at[head, i], (c, h)
            ).wait_recv()
            part_copy(head, i, lax.rem(me + off, 4)).wait_send()
        attention[:, pl.ds(head * HD, HD)] = merge_attention(parts_in.at[head]).T.astype(BF16)

    for load in loads[19:27]:
        load.wait()

    def out_terms(block):
        return jnp.dot(attention[...], wo[block], preferred_element_type=F32)

    def scatter(which, produce):
        return scatter_sums(
            ring,
            produce,
            sib_out.at[which],
            sib_in.at[which],
            far_out.at[which],
            far_in.at[which],
            near_out.at[which],
            near_in.at[which],
            sum_ssem.at[which],
            sum_rsem.at[which],
        )

    attn_own[...] = scatter(0, out_terms)
    rows_mid[pl.ds(h, 1)] = (
        (rows_in[pl.ds(h, 1)].astype(F32) + attn_own[...][None]).astype(BF16)
    )

    acc_gate[...] = jnp.zeros_like(acc_gate)
    acc_up[...] = jnp.zeros_like(acc_up)
    squares[...] = jnp.zeros_like(squares)
    for load in loads[3:19]:
        load.wait()

    def absorb_middle(block):
        wide = rows_mid[block].astype(F32)
        squares[...] += lane_sum(wide * wide)
        scaled = (wide * gain_ffn[block]).astype(BF16)
        acc_gate[...] += dot_rows(scaled, wg[block])
        acc_up[...] += dot_rows(scaled, wu[block])

    gather_blocks(ring, rows_mid, gather_ssem.at[1], gather_rsem.at[1], absorb_middle)
    scale_ffn = lax.rsqrt(jnp.sum(squares[...], axis=1, keepdims=True) * (1.0 / FULL) + EPS)
    gate = acc_gate[...] * scale_ffn
    hidden[...] = (gate / (1.0 + jnp.exp(-gate)) * (acc_up[...] * scale_ffn)).astype(BF16)

    for load in loads[27:35]:
        load.wait()

    def down_terms(block):
        return jnp.dot(hidden[...], wd[block], preferred_element_type=F32)

    ffn_own = scatter(1, down_terms)
    own = rows_in[pl.ds(h, 1)][0].astype(F32)
    out[...] = (own + router * (attn_own[...] + ffn_own)).astype(BF16)


def body(
    chosen,
    positions,
    counts,
    w_router,
    gain_attn,
    query_weight,
    w_key,
    w_value,
    w_out,
    gain_ffn,
    w_gate,
    w_up,
    w_down,
):
    del positions
    units = w_gate.shape[1]
    vmem = pl.BlockSpec(memory_space=pltpu.VMEM)
    smem = pl.BlockSpec(memory_space=pltpu.SMEM)
    hbm = pl.BlockSpec(memory_space=pl.ANY)
    dma = pltpu.SemaphoreType.DMA
    result = pl.pallas_call(
        block_kernel,
        out_shape=jax.ShapeDtypeStruct((ROWS, WIDTH), BF16),
        in_specs=[smem, vmem, vmem, vmem, hbm, hbm, hbm, hbm, vmem, hbm, hbm, hbm],
        out_specs=vmem,
        scratch_shapes=[
            pltpu.VMEM((8, WIDTH, 2 * HD), BF16),
            pltpu.VMEM((8, WIDTH, 2 * HD), BF16),
            pltpu.VMEM((8, WIDTH, 2 * HD), BF16),
            pltpu.VMEM((8, 2 * HD, WIDTH), BF16),
            pltpu.VMEM((8, units, WIDTH), BF16),
            pltpu.VMEM((8, units, WIDTH), BF16),
            pltpu.VMEM((8, units, WIDTH), BF16),
            pltpu.VMEM((16, 32, WIDTH), BF16),
            pltpu.VMEM((16, 32, WIDTH), BF16),
            pltpu.VMEM((8, ROWS, WIDTH), BF16),
            pltpu.VMEM((8, ROWS, WIDTH), BF16),
            pltpu.VMEM((ROWS, 6 * HD), F32),
            pltpu.VMEM((ROWS, 128), F32),
            pltpu.VMEM((ROWS, 128), F32),
            pltpu.VMEM((4, PACK, HD), BF16),
            pltpu.VMEM((4, PACK, HD), BF16),
            pltpu.VMEM((2, 4, ROWS, ROWS), F32),
            pltpu.VMEM((2, 4, OUT_ROWS, ROWS), BF16),
            pltpu.VMEM((2, 4, OUT_ROWS, ROWS), BF16),
            pltpu.VMEM((ROWS, 2 * HD), BF16),
            pltpu.VMEM((ROWS, units), F32),
            pltpu.VMEM((ROWS, units), F32),
            pltpu.VMEM((ROWS, units), BF16),
            pltpu.VMEM((ROWS, WIDTH), F32),
            pltpu.VMEM((2, 4, ROWS, WIDTH), BF16),
            pltpu.VMEM((2, 4, ROWS, WIDTH), BF16),
            pltpu.VMEM((2, ROWS, WIDTH), BF16),
            pltpu.VMEM((2, ROWS, WIDTH), BF16),
            pltpu.VMEM((2, 2, ROWS, WIDTH), BF16),
            pltpu.VMEM((2, 2, ROWS, WIDTH), BF16),
            dma((35,)),
            dma((16,)),
            dma((16,)),
            dma((2, 10)),
            dma((2, 10)),
            dma((2, 6)),
            dma((2, 6)),
            dma((2, 3)),
            dma((2, 3)),
            dma((2, 10)),
            dma((2, 10)),
        ],
        compiler_params=pltpu.CompilerParams(
            collective_id=0, has_side_effects=True, vmem_limit_bytes=60 * 1024 * 1024
        ),
        cost_estimate=pl.CostEstimate(
            flops=9_000_000_000, bytes_accessed=30_000_000, transcendentals=3_000_000
        ),
    )(
        counts,
        chosen,
        w_router.reshape(8, 1, WIDTH),
        gain_attn.reshape(8, 1, WIDTH),
        query_weight.reshape(8, WIDTH, 2 * HD),
        w_key.reshape(8, WIDTH, 2 * HD),
        w_value.reshape(8, WIDTH, 2 * HD),
        w_out,
        gain_ffn.reshape(8, 1, WIDTH),
        w_gate.T,
        w_up.T,
        w_down,
    )
    return result.reshape(1, ROWS, WIDTH)


def solution(mesh):
    in_specs = (
        P("ctx", "head"),
        P("ctx"),
        P(),
        P(),
        P(),
        P(None, "head"),
        P(None, "head"),
        P(None, "head"),
        P("head", None),
        P(),
        P(None, "head"),
        P(None, "head"),
        P("head", None),
    )
    out_specs = P("ctx", None, "head")
    return jax.shard_map(body, mesh=mesh, in_specs=in_specs, out_specs=out_specs, check_vma=False)
```
